32 devices in a mesh: leaf: 4 (over y, x), row: 4 (over z), col: 2 (over core).
Axes of the slice: x: 2, y: 2, z: 4, core: 2. Of those that a mesh axis runs over, the one named last changes fastest.
Arguments:
- local_inv: float32 [4, 4, 32, 128, 128], P('leaf', 'row', 'col'), may hold values from -2 to 2, as said below
- local_off: float32 [4, 4, 32, 2, 128, 128], P('leaf', 'row', 'col'), may hold values from -0.09375 to 0.09375
- local_dep: int32 [4, 4, 32, 2], P('leaf', 'row', 'col'), may hold values from 0 to 7
- local_rhs: float32 [4, 4, 32, 64, 128], P('leaf', 'row', 'col'), may hold values from -6 to 6
- top_inv: float32 [8, 4, 2, 128, 128], P(None, 'row', 'col'), may hold values from -2 to 2, as said below
- top_off: float32 [7, 4, 2, 4, 128, 128], P(None, 'row', 'col'), may hold values from -0.125 to 0.125
- top_dep: int32 [7, 4, 2, 4], P(None, 'row', 'col'), may hold values from 0 to 5
- top_rhs: float32 [8, 4, 2, 64, 128], P(None, 'row', 'col'), may hold values from -6 to 6
Outputs:
- local_sol: float32 [4, 4, 32, 64, 128], P('leaf', 'row', 'col')
- top_sol: float32 [8, 4, 2, 64, 128], P(None, 'row', 'col')
The draws below stay inside these ranges and needn't reach their ends.
Inputs may be any that keep to these rules, and one draw needn't show every extreme that they name: `local_inv`: lower-triangular inverse diagonal blocks of a Cholesky factor: entry [t, s] is zero for s > t. `top_inv`: lower-triangular inverse diagonal blocks of a Cholesky factor: entry [t, s] is zero for s > t. `local_dep`: levels of ancestors owned by the supernode's own grid cell. `top_dep`: a value v < 2 names the supernode one level lower in cell (r, v); a value v >= 2 the one in cell (v - 2, c).
All inputs are finite; a program needn't handle non-finite values.
Results may differ from the reference program's by a relative error of at most 0.0001.
Values sent between devices are 32-bit elements; how exact they have to be, the bound alone decides.
A program may use at most 64 MiB of HBM per device.

```python
import jax
import jax.numpy as jnp
from jax import lax

S = 128
R = 64
LOC = 16
FAN = 2
DEP = 4
LEVELS = 8
N_LEAF = 4
N_ROW = 4
N_COL = 2


def inverse_blocks(key, shape):
    key_off, key_diag = jax.random.split(key)
    identity = jnp.eye(S, dtype=jnp.float32)
    lower = (jnp.arange(S)[:, None] > jnp.arange(S)[None, :]).astype(jnp.float32)
    spread = jax.random.normal(key_off, shape, jnp.float32) * (0.8 / S ** 0.5)
    diagonal = jax.random.uniform(key_diag, shape[:-1], jnp.float32, 0.5, 1.5)
    return spread * lower + diagonal[..., None] * identity


def draw_local_inv(key, part):
    return inverse_blocks(jax.random.fold_in(key, 11), (N_LEAF, N_ROW, N_COL * LOC, S, S))


def draw_top_inv(key, part):
    return inverse_blocks(jax.random.fold_in(key, 23), (LEVELS, N_ROW, N_COL, S, S))


def plant(values, rng, low, top_value):
    dims = values.shape
    spot = [jax.random.randint(jax.random.fold_in(rng, axis), (), 0, dims[axis]) for axis in range(len(dims))]
    values = values.at[tuple(spot)].set(low)
    longest = dims.index(max(dims))
    spot[longest] = (spot[longest] + 1) % dims[longest]
    return values.at[tuple(spot)].set(top_value)


def block_levels(rng, shape, shards, smallest, top_value):
    factor_of, own = 1.0, jax.random.fold_in(rng, 6)
    for axis_at, parts in shards:
        steps = jnp.exp(jax.random.uniform(jax.random.fold_in(own, axis_at), (parts,), jnp.float32, smallest / len(shards), top_value / len(shards)))
        factor_of = factor_of * jnp.repeat(steps, shape[axis_at] // parts).reshape([-1 if axis == axis_at else 1 for axis in range(len(shape))])
    return factor_of


def scatter_about(rng, dims, scale, reach, cuts=(), held_as=jnp.bfloat16):
    array = scale * jax.random.normal(rng, dims, jnp.float32)
    if cuts:
        array = array * block_levels(rng, dims, cuts, -0.22, 0.18)
    return jnp.clip(array, -reach, reach).astype(held_as)


def setup_inputs(seed: int = 0) -> dict:
    keys = jax.random.split(jax.random.key(seed), 9)
    local_inv = draw_local_inv(jax.random.fold_in(keys[8], 71), 0)
    local_off = scatter_about(keys[1], (N_LEAF, N_ROW, N_COL * LOC, FAN, S, S), (S * LOC * FAN) ** -0.5, 0.09375, ((0, 4), (1, 4), (2, 2)), jnp.float32)
    local_dep = plant(jax.random.randint(keys[2], (N_LEAF, N_ROW, N_COL * LOC, FAN), 0, LEVELS), jax.random.fold_in(keys[2], 1), 0, LEVELS - 1).astype(jnp.int32)
    local_rhs = scatter_about(keys[3], (N_LEAF, N_ROW, N_COL * LOC, R, S), 1.0, 6.0, ((0, 4), (1, 4), (2, 2)), jnp.float32)
    top_inv = draw_top_inv(jax.random.fold_in(keys[8], 71), 0)
    top_off = scatter_about(keys[5], (LEVELS - 1, N_ROW, N_COL, DEP, S, S), (4 * DEP * S) ** -0.5, 0.125, ((1, 4), (2, 2)), jnp.float32)
    top_dep = plant(jax.random.randint(keys[6], (LEVELS - 1, N_ROW, N_COL, DEP), 0, N_COL + N_ROW), jax.random.fold_in(keys[6], 1), 0, (N_COL + N_ROW) - 1).astype(jnp.int32)
    top_rhs = scatter_about(keys[7], (LEVELS, N_ROW, N_COL, R, S), 1.0, 6.0, ((1, 4), (2, 2)), jnp.float32)
    return dict(local_inv=local_inv, local_off=local_off, local_dep=local_dep, local_rhs=local_rhs, top_inv=top_inv, top_off=top_off, top_dep=top_dep, top_rhs=top_rhs)


highest = lax.Precision.HIGHEST


def reference(local_inv, local_off, local_dep, local_rhs, top_inv, top_off, top_dep, top_rhs):
    inverse = local_inv.reshape(N_LEAF, N_ROW, N_COL, LOC, S, S)
    blocks = local_off.reshape(N_LEAF, N_ROW, N_COL, LOC, FAN, S, S)
    ancestor_levels = local_dep.reshape(N_LEAF, N_ROW, N_COL, LOC, FAN)
    right_local = local_rhs.reshape(N_LEAF, N_ROW, N_COL, LOC, R, S)
    local_first = jnp.einsum('abckrs,abckts->abckrt', right_local, inverse, precision=highest)
    matches = (ancestor_levels[..., None] == jnp.arange(LEVELS, dtype=jnp.int32)).astype(jnp.float32)
    contributions = jnp.einsum('abckrs,abckjts->abckjrt', local_first, blocks, precision=highest)
    updates = jnp.einsum('abckjl,abckjrt->lbcrt', matches, contributions, precision=highest)
    forward = []
    for height in range(LEVELS):
        target = top_rhs[height] - updates[height]
        if height > 0:
            latest = forward[-1]
            cand_cols = jnp.broadcast_to(latest[:, None], (N_ROW, N_COL, N_COL, R, S))
            cand_rows = jnp.broadcast_to(jnp.transpose(latest, (1, 0, 2, 3))[None], (N_ROW, N_COL, N_ROW, R, S))
            candidates = jnp.concatenate([cand_cols, cand_rows], axis=2)
            picks = (top_dep[height - 1][..., None] == jnp.arange(N_COL + N_ROW, dtype=jnp.int32)).astype(jnp.float32)
            picked = jnp.einsum('abjv,abvrs->abjrs', picks, candidates, precision=highest)
            target = target - jnp.einsum('abjrs,abjts->abrt', picked, top_off[height - 1], precision=highest)
        forward.append(jnp.einsum('abrs,abts->abrt', target, top_inv[height], precision=highest))
    backward = [None] * LEVELS
    current = jnp.einsum('abrs,abst->abrt', forward[LEVELS - 1], top_inv[LEVELS - 1], precision=highest)
    backward[LEVELS - 1] = current
    for height in range(LEVELS - 2, -1, -1):
        pieces = jnp.einsum('abrt,abjts->abjrs', current, top_off[height], precision=highest)
        sources = top_dep[height]
        to_cols = (sources[..., None] == jnp.arange(N_COL, dtype=jnp.int32)).astype(jnp.float32)
        to_rows = (sources[..., None] == N_COL + jnp.arange(N_ROW, dtype=jnp.int32)).astype(jnp.float32)
        incoming = jnp.einsum('abjv,abjrs->avrs', to_cols, pieces, precision=highest)
        incoming = incoming + jnp.einsum('abju,abjrs->ubrs', to_rows, pieces, precision=highest)
        current = jnp.einsum('abrs,abst->abrt', forward[height] - incoming, top_inv[height], precision=highest)
        backward[height] = current
    top_solution = jnp.stack(backward)
    ancestors = jnp.einsum('abckjl,lbcrt->abckjrt', matches, top_solution, precision=highest)
    remainder = local_first - jnp.einsum('abckjrt,abckjts->abckrs', ancestors, blocks, precision=highest)
    local_solution = jnp.einsum('abckrs,abckst->abckrt', remainder, inverse, precision=highest)
    return local_solution.reshape(N_LEAF, N_ROW, N_COL * LOC, R, S), top_solution
```

```python
import functools

import jax
import jax.numpy as jnp
from jax import lax
from jax.experimental import pallas as pl
from jax.experimental.pallas import tpu as pltpu
from jax.sharding import PartitionSpec as P

MESH = pl.DeviceIdType.MESH
f32 = jnp.float32
bf16 = jnp.bfloat16
NN = (((1,), (0,)), ((), ()))
NT = (((1,), (1,)), ((), ()))


def split(x):
    high = x.astype(bf16)
    return high, (x - high.astype(f32)).astype(bf16)


def dot3(a, b, dims):
    rows = a.shape[0]
    ah, al = split(a)
    bh, bl = b
    both = lax.dot_general(jnp.concatenate([ah, al], axis=0), bh, dims, preferred_element_type=f32)
    cross = lax.dot_general(ah, bl, dims, preferred_element_type=f32)
    return both[:rows] + both[rows:] + cross


def kernel(
    sizes, chunk,
    ldep, tdep, inv_h, off_h, rhs_h, tinv_h, toff_h, trhs_h,
    lsol_h, tsol_h,
    inv, off, rhs, tinv, toff, trhs, first, upd, rs, ybuf, yown, bout, bin_, tsol, lsol,
    wh, wl, vh, vl,
    in_sem, out_sem, rs_send, rs_recv, f_send, f_recv, b_send, b_recv, ag_send, ag_recv,
):
    n_leaf, n_row, n_col = sizes
    loc, s = inv.shape[0], inv.shape[1]
    fan = off.shape[1] // s
    levels, r = upd.shape[0], upd.shape[1]
    dep = tdep.shape[1]
    part = r // n_leaf
    slots = n_col + n_row
    q, me_r, me_c = lax.axis_index("leaf"), lax.axis_index("row"), lax.axis_index("col")
    leaf_peers = [lax.rem(q + d, n_leaf) for d in range(1, n_leaf)]
    row_peers = [lax.rem(me_r + d, n_row) for d in range(1, n_row)]
    col_peers = [lax.rem(me_c + d, n_col) for d in range(1, n_col)]
    at_leaf = [(p, me_r, me_c) for p in leaf_peers]
    at_row = [(q, p, me_c) for p in row_peers]
    at_col = [(q, me_r, p) for p in col_peers]

    def rows_of(p):
        return pl.ds(pl.multiple_of(p * part, part), part)

    mine = rows_of(q)

    n_chunks = loc // chunk
    loads = []
    for c in range(n_chunks):
        ks = pl.ds(c * chunk, chunk)
        for place, (src, dst) in enumerate(((rhs_h, rhs), (inv_h, inv), (off_h, off))):
            loads.append(pltpu.make_async_copy(src.at[ks], dst.at[ks], in_sem.at[3 * c + place]))
    late = 3 * n_chunks
    top_loads = [
        pltpu.make_async_copy(tinv_h, tinv, in_sem.at[late]),
        pltpu.make_async_copy(trhs_h.at[:, mine], trhs, in_sem.at[late + 1]),
        pltpu.make_async_copy(toff_h, toff, in_sem.at[late + 2]),
    ]
    for load in loads + top_loads:
        load.start()

    barrier = pltpu.get_barrier_semaphore()
    for peer in at_leaf + at_row + at_col:
        pl.semaphore_signal(barrier, inc=1, device_id=peer, device_id_type=MESH)

    for c in range(n_chunks):
        for load in loads[3 * c:3 * c + 3]:
            load.wait()
        contributions = []
        for k in range(c * chunk, (c + 1) * chunk):
            y = dot3(rhs[k], split(inv[k]), NT)
            first[k] = y
            both = dot3(y, split(off[k]), NT)
            for j in range(fan):
                contributions.append((ldep[k, j], both[:, j * s:(j + 1) * s]))
        for l in range(levels):
            total = None
            for level, block in contributions:
                term = jnp.where(level == l, 1.0, 0.0) * block
                total = term if total is None else total + term
            upd[l] = total if c == 0 else upd[l] + total

    pl.semaphore_wait(barrier, n_leaf + n_row + n_col - 3)

    def rs_copy(half, p, slot, device):
        ls = pl.ds(0, 1) if half == 0 else pl.ds(1, levels - 1)
        return pltpu.make_async_remote_copy(
            src_ref=upd.at[ls, rows_of(p)], dst_ref=rs.at[slot, ls],
            send_sem=rs_send.at[half, p], recv_sem=rs_recv.at[half, slot],
            device_id=device, device_id_type=MESH,
        )

    for half in range(2):
        for p, device in zip(leaf_peers, at_leaf):
            rs_copy(half, p, q, device).start()
    rs[q] = upd[:, mine]

    def local_fold(k):
        both = dot3(jnp.concatenate([off[k], first[k]], axis=0), split(inv[k]), NN)
        high, low = split(both[:fan * s])
        vh[k] = high
        vl[k] = low
        first[k] = both[fan * s:]

    for load in top_loads:
        load.wait()
    per_gap = loc // (levels - 1)
    early = loc - per_gap * (levels - 1)
    for k in range(early):
        local_fold(k)

    def rs_wait(half):
        for p, device in zip(leaf_peers, at_leaf):
            rs_copy(half, p, p, device).wait_recv()

    def own_part(l):
        z = trhs[l]
        for p in range(n_leaf):
            z = z - rs[p, l]
        return dot3(z, split(tinv[l]), NT)

    def f_copy(l, slot, device):
        return pltpu.make_async_remote_copy(
            src_ref=ybuf.at[l, slot], dst_ref=ybuf.at[l, slot],
            send_sem=f_send.at[l, device[0]], recv_sem=f_recv.at[l, slot],
            device_id=device[1], device_id_type=MESH,
        )

    col_out = [(p, d) for p, d in zip(col_peers, at_col)]
    row_out = [(n_col + p, d) for p, d in zip(row_peers, at_row)]

    def f_start(l, y):
        ybuf[l, me_c] = y
        ybuf[l, n_col + me_r] = y
        for target in row_out:
            f_copy(l, n_col + me_r, target).start()
        for target in col_out:
            f_copy(l, me_c, target).start()

    rs_wait(0)
    y = own_part(0)
    yown[0] = y
    f_start(0, y)
    rs_wait(1)

    def fold(l):
        inverse = tinv[l]
        for j in range(dep):
            high, low = split(dot3(inverse, split(toff[l - 1, j * s:(j + 1) * s]), NN))
            wh[l - 1, :, j * s:(j + 1) * s] = high
            wl[l - 1, :, j * s:(j + 1) * s] = low

    def up(l, y):
        fold(l)
        own = own_part(l)
        picks = [
            [jnp.where(tdep[l - 1, j] == slot, 1.0, 0.0) for slot in range(slots)]
            for j in range(dep)
        ]
        for slot, device in col_out + row_out:
            f_copy(l - 1, slot, (slot, device)).wait_recv()
        blocks = [ybuf[l - 1, slot] for slot in range(slots)]
        picked = []
        for j in range(dep):
            total = None
            for slot in range(slots):
                term = picks[j][slot] * blocks[slot]
                total = term if total is None else total + term
            picked.append(total)
        return own - dot3(jnp.concatenate(picked, axis=1), (wh[l - 1], wl[l - 1]), NT)

    def forward(l, y):
        y = up(l, y)
        yown[l] = y
        f_start(l, y)
        return y

    y = lax.fori_loop(1, levels - 1, forward, y)
    d = up(levels - 1, y)

    def ag_copy(l, p, owner, device):
        return pltpu.make_async_remote_copy(
            src_ref=tsol.at[l, rows_of(owner)], dst_ref=tsol.at[l, rows_of(owner)],
            send_sem=ag_send.at[l, p], recv_sem=ag_recv.at[l, owner],
            device_id=device, device_id_type=MESH,
        )

    def publish(l, d):
        tsol[l, mine] = dot3(d, split(tinv[l]), NN)
        for p, device in zip(leaf_peers, at_leaf):
            ag_copy(l, p, q, device).start()

    def b_copy(l, slot, landing, device):
        return pltpu.make_async_remote_copy(
            src_ref=bout.at[l, slot], dst_ref=bin_.at[l, landing],
            send_sem=b_send.at[l, slot], recv_sem=b_recv.at[l, landing],
            device_id=device, device_id_type=MESH,
        )

    def backward(step, d):
        l = levels - 1 - step
        pieces = dot3(d, (wh[l - 1], wl[l - 1]), NN)
        sources = [tdep[l - 1, j] for j in range(dep)]
        for slot in range(slots):
            total = None
            for j in range(dep):
                term = jnp.where(sources[j] == slot, 1.0, 0.0) * pieces[:, j * s:(j + 1) * s]
                total = term if total is None else total + term
            bout[l - 1, slot] = total
        for slot, device in row_out:
            b_copy(l - 1, slot, n_col + me_r, device).start()
        for slot, device in col_out:
            b_copy(l - 1, slot, me_c, device).start()
        bin_[l - 1, me_c] = bout[l - 1, me_c]
        bin_[l - 1, n_col + me_r] = bout[l - 1, n_col + me_r]
        publish(l, d)
        for extra in range(per_gap):
            local_fold(early + step * per_gap + extra)
        for slot, device in col_out + row_out:
            b_copy(l - 1, slot, slot, device).wait_recv()
        total = bin_[l - 1, 0]
        for slot in range(1, slots):
            total = total + bin_[l - 1, slot]
        return yown[l - 1] - total

    d = lax.fori_loop(0, levels - 1, backward, d)
    publish(0, d)

    def ag_wait(l, carry):
        for p, device in zip(leaf_peers, at_leaf):
            ag_copy(l, p, p, device).wait_recv()
        return carry

    lax.fori_loop(0, levels, ag_wait, 0)
    top_out = pltpu.make_async_copy(tsol, tsol_h, out_sem.at[n_chunks])
    top_out.start()

    outs = []
    for c in range(n_chunks):
        ks = pl.ds(c * chunk, chunk)
        for k in range(c * chunk, (c + 1) * chunk):
            above = jnp.concatenate([tsol[ldep[k, j]] for j in range(fan)], axis=1)
            lsol[k] = first[k] - dot3(above, (vh[k], vl[k]), NN)
        outs.append(pltpu.make_async_copy(lsol.at[ks], lsol_h.at[ks], out_sem.at[c]))
        outs[-1].start()

    for half in range(2):
        for p, device in zip(leaf_peers, at_leaf):
            rs_copy(half, p, q, device).wait_send()

    def drain(l, carry):
        for target in row_out:
            f_copy(l, n_col + me_r, target).wait_send()
        for target in col_out:
            f_copy(l, me_c, target).wait_send()
        for slot, device in row_out + col_out:
            b_copy(l, slot, slot, device).wait_send()
        return carry

    lax.fori_loop(0, levels - 1, drain, 0)

    def drain_ag(l, carry):
        for p, device in zip(leaf_peers, at_leaf):
            ag_copy(l, p, q, device).wait_send()
        return carry

    lax.fori_loop(0, levels, drain_ag, 0)
    for out in outs + [top_out]:
        out.wait()


def on_device(sizes, local_inv, local_off, local_dep, local_rhs, top_inv, top_off, top_dep, top_rhs):
    n_leaf, n_row, n_col = sizes
    loc, s = local_inv.shape[2], local_inv.shape[3]
    fan = local_off.shape[3]
    r = local_rhs.shape[3]
    levels, dep = top_inv.shape[0], top_off.shape[3]
    part, slots = r // n_leaf, n_row + n_col
    chunk = 4 if loc % 4 == 0 else 1
    n_chunks = loc // chunk
    hbm = pl.BlockSpec(memory_space=pl.ANY)
    smem = pl.BlockSpec(memory_space=pltpu.SMEM)
    dma = pltpu.SemaphoreType.DMA
    local_sol, top_sol = pl.pallas_call(
        functools.partial(kernel, sizes, chunk),
        out_shape=(
            jax.ShapeDtypeStruct((loc, r, s), f32),
            jax.ShapeDtypeStruct((levels, r, s), f32),
        ),
        in_specs=[smem, smem] + [hbm] * 6,
        out_specs=(hbm, hbm),
        scratch_shapes=[
            pltpu.VMEM((loc, s, s), f32),
            pltpu.VMEM((loc, fan * s, s), f32),
            pltpu.VMEM((loc, r, s), f32),
            pltpu.VMEM((levels, s, s), f32),
            pltpu.VMEM((levels - 1, dep * s, s), f32),
            pltpu.VMEM((levels, part, s), f32),
            pltpu.VMEM((loc, r, s), f32),
            pltpu.VMEM((levels, r, s), f32),
            pltpu.VMEM((n_leaf, levels, part, s), f32),
            pltpu.VMEM((levels - 1, slots, part, s), f32),
            pltpu.VMEM((levels, part, s), f32),
            pltpu.VMEM((levels - 1, slots, part, s), f32),
            pltpu.VMEM((levels - 1, slots, part, s), f32),
            pltpu.VMEM((levels, r, s), f32),
            pltpu.VMEM((loc, r, s), f32),
            pltpu.VMEM((levels - 1, s, dep * s), bf16),
            pltpu.VMEM((levels - 1, s, dep * s), bf16),
            pltpu.VMEM((loc, fan * s, s), bf16),
            pltpu.VMEM((loc, fan * s, s), bf16),
            dma((3 * n_chunks + 3,)),
            dma((n_chunks + 1,)),
            dma((2, n_leaf)),
            dma((2, n_leaf)),
            dma((levels - 1, slots)),
            dma((levels - 1, slots)),
            dma((levels - 1, slots)),
            dma((levels - 1, slots)),
            dma((levels, n_leaf)),
            dma((levels, n_leaf)),
        ],
        compiler_params=pltpu.CompilerParams(
            collective_id=0, has_side_effects=True, vmem_limit_bytes=40 * 2**20
        ),
    )(
        local_dep.reshape(loc, fan),
        top_dep.reshape(levels - 1, dep),
        local_inv.reshape(loc, s, s),
        local_off.reshape(loc, fan * s, s),
        local_rhs.reshape(loc, r, s),
        top_inv.reshape(levels, s, s),
        top_off.reshape(levels - 1, dep * s, s),
        top_rhs.reshape(levels, r, s),
    )
    return local_sol[None, None], top_sol[:, None, None]


def solution(mesh):
    placed = (
        P("leaf", "row", "col", None, None),
        P("leaf", "row", "col", None, None, None),
        P("leaf", "row", "col", None),
        P("leaf", "row", "col", None, None),
        P(None, "row", "col", None, None),
        P(None, "row", "col", None, None, None),
        P(None, "row", "col", None),
        P(None, "row", "col", None, None),
    )
    sizes = (mesh.shape["leaf"], mesh.shape["row"], mesh.shape["col"])
    return jax.shard_map(
        functools.partial(on_device, sizes),
        mesh=mesh,
        in_specs=placed,
        out_specs=(P("leaf", "row", "col", None, None), P(None, "row", "col", None, None)),
        check_vma=False,
    )
```

```python
import functools

import jax
import jax.numpy as jnp
from jax import lax
from jax.experimental import pallas as pl
from jax.experimental.pallas import tpu as pltpu
from jax.sharding import PartitionSpec as P

MESH = pl.DeviceIdType.MESH
f32 = jnp.float32
bf16 = jnp.bfloat16
NN = (((1,), (0,)), ((), ()))
NT = (((1,), (1,)), ((), ()))


def split(x):
    high = x.astype(bf16)
    return high, (x - high.astype(f32)).astype(bf16)


def dot3(a, b, dims):
    rows = a.shape[0]
    ah, al = split(a)
    bh, bl = b
    both = lax.dot_general(jnp.concatenate([ah, al], axis=0), bh, dims, preferred_element_type=f32)
    cross = lax.dot_general(ah, bl, dims, preferred_element_type=f32)
    return both[:rows] + both[rows:] + cross


def farthest_first(me, n):
    upper = (2 * me) // n
    peers = []
    for i in range(n - 1):
        up = i + jnp.where(i >= me, 1, 0)
        down = n - 1 - i - jnp.where(n - 1 - i <= me, 1, 0)
        peers.append(upper * up + (1 - upper) * down)
    return peers


def kernel(
    sizes, chunk,
    ldep, tdep, inv_h, off_h, rhs_h, tinv_h, toff_h, trhs_h,
    lsol_h, tsol_h,
    inv, off, rhs, tinv, toff, trhs, first, upd, rs, ybuf, yown, bout, bin_, tsol, lsol,
    wh, wl, vh, vl,
    in_sem, out_sem, rs_send, rs_recv, f_send, f_recv, b_send, b_recv, ag_send, ag_recv,
):
    n_leaf, n_row, n_col = sizes
    loc, s = inv.shape[0], inv.shape[1]
    fan = off.shape[1] // s
    levels, r = upd.shape[0], upd.shape[1]
    dep = tdep.shape[0]
    part = r // n_leaf
    slots = n_col + n_row
    q, me_r, me_c = lax.axis_index("leaf"), lax.axis_index("row"), lax.axis_index("col")
    leaf_peers = [lax.rem(q + d, n_leaf) for d in range(1, n_leaf)]
    row_peers = farthest_first(me_r, n_row)
    col_peers = [lax.rem(me_c + d, n_col) for d in range(1, n_col)]
    at_leaf = [(p, me_r, me_c) for p in leaf_peers]
    at_row = [(q, p, me_c) for p in row_peers]
    at_col = [(q, me_r, p) for p in col_peers]

    def rows_of(p):
        return pl.ds(pl.multiple_of(p * part, part), part)

    mine = rows_of(q)

    n_chunks = loc // chunk
    loads = []
    for c in range(n_chunks):
        ks = pl.ds(c * chunk, chunk)
        for place, (src, dst) in enumerate(((rhs_h, rhs), (inv_h, inv), (off_h, off))):
            loads.append(pltpu.make_async_copy(src.at[ks], dst.at[ks], in_sem.at[3 * c + place]))
    late = 3 * n_chunks
    top_loads = [
        pltpu.make_async_copy(tinv_h, tinv, in_sem.at[late]),
        pltpu.make_async_copy(trhs_h.at[:, mine], trhs, in_sem.at[late + 1]),
        pltpu.make_async_copy(toff_h, toff, in_sem.at[late + 2]),
    ]
    for load in loads + top_loads:
        load.start()

    barrier = pltpu.get_barrier_semaphore()
    for peer in at_leaf + at_row + at_col:
        pl.semaphore_signal(barrier, inc=1, device_id=peer, device_id_type=MESH)

    for c in range(n_chunks):
        for load in loads[3 * c:3 * c + 3]:
            load.wait()
        contributions = []
        for k in range(c * chunk, (c + 1) * chunk):
            y = dot3(rhs[k], split(inv[k]), NT)
            first[k] = y
            both = dot3(y, split(off[k]), NT)
            for j in range(fan):
                contributions.append((ldep[j, k], both[:, j * s:(j + 1) * s]))
        for l in range(levels):
            total = None
            for level, block in contributions:
                term = jnp.where(level == l, 1.0, 0.0) * block
                total = term if total is None else total + term
            upd[l] = total if c == 0 else upd[l] + total

    pl.semaphore_wait(barrier, n_leaf + n_row + n_col - 3)

    def rs_copy(half, p, slot, device):
        ls = pl.ds(0, 1) if half == 0 else pl.ds(1, levels - 1)
        return pltpu.make_async_remote_copy(
            src_ref=upd.at[ls, rows_of(p)], dst_ref=rs.at[slot, ls],
            send_sem=rs_send.at[half, p], recv_sem=rs_recv.at[half, slot],
            device_id=device, device_id_type=MESH,
        )

    for half in range(2):
        for p, device in zip(leaf_peers, at_leaf):
            rs_copy(half, p, q, device).start()
    rs[q] = upd[:, mine]

    def local_fold(k):
        both = dot3(jnp.concatenate([off[k], first[k]], axis=0), split(inv[k]), NN)
        high, low = split(both[:fan * s])
        vh[k] = high
        vl[k] = low
        first[k] = both[fan * s:]

    for load in top_loads:
        load.wait()
    per_gap = loc // (levels - 1)
    early = loc - per_gap * (levels - 1)
    for k in range(early):
        local_fold(k)

    def rs_wait(half):
        for p, device in zip(leaf_peers, at_leaf):
            rs_copy(half, p, p, device).wait_recv()

    def own_part(l):
        z = trhs[l]
        for p in range(n_leaf):
            z = z - rs[p, l]
        return dot3(z, split(tinv[l]), NT)

    def f_copy(l, slot, device):
        return pltpu.make_async_remote_copy(
            src_ref=ybuf.at[l, slot], dst_ref=ybuf.at[l, slot],
            send_sem=f_send.at[l, device[0]], recv_sem=f_recv.at[l, slot],
            device_id=device[1], device_id_type=MESH,
        )

    col_out = [(p, d) for p, d in zip(col_peers, at_col)]
    row_out = [(n_col + p, d) for p, d in zip(row_peers, at_row)]

    def f_start(l, y):
        ybuf[l, me_c] = y
        ybuf[l, n_col + me_r] = y
        for target in row_out:
            f_copy(l, n_col + me_r, target).start()
        for target in col_out:
            f_copy(l, me_c, target).start()

    rs_wait(0)
    y = own_part(0)
    yown[0] = y
    f_start(0, y)
    rs_wait(1)

    def fold(l):
        inverse = tinv[l]
        for j in range(dep):
            high, low = split(dot3(inverse, split(toff[l - 1, j * s:(j + 1) * s]), NN))
            wh[l - 1, :, j * s:(j + 1) * s] = high
            wl[l - 1, :, j * s:(j + 1) * s] = low

    def up(l, y):
        fold(l)
        own = own_part(l)
        picks = [
            [jnp.where(tdep[j, l - 1] == slot, 1.0, 0.0) for slot in range(slots)]
            for j in range(dep)
        ]
        for slot, device in col_out + row_out:
            f_copy(l - 1, slot, (slot, device)).wait_recv()
        blocks = [ybuf[l - 1, slot] for slot in range(slots)]
        picked = []
        for j in range(dep):
            total = None
            for slot in range(slots):
                term = picks[j][slot] * blocks[slot]
                total = term if total is None else total + term
            picked.append(total)
        return own - dot3(jnp.concatenate(picked, axis=1), (wh[l - 1], wl[l - 1]), NT)

    def forward(l, y):
        y = up(l, y)
        yown[l] = y
        f_start(l, y)
        return y

    y = lax.fori_loop(1, levels - 1, forward, y)
    d = up(levels - 1, y)

    def ag_copy(l, p, owner, device):
        return pltpu.make_async_remote_copy(
            src_ref=tsol.at[l, rows_of(owner)], dst_ref=tsol.at[l, rows_of(owner)],
            send_sem=ag_send.at[l, p], recv_sem=ag_recv.at[l, owner],
            device_id=device, device_id_type=MESH,
        )

    def publish(l, d):
        tsol[l, mine] = dot3(d, split(tinv[l]), NN)
        for p, device in zip(leaf_peers, at_leaf):
            ag_copy(l, p, q, device).start()

    def b_copy(l, slot, landing, device):
        return pltpu.make_async_remote_copy(
            src_ref=bout.at[l, slot], dst_ref=bin_.at[l, landing],
            send_sem=b_send.at[l, slot], recv_sem=b_recv.at[l, landing],
            device_id=device, device_id_type=MESH,
        )

    def backward(step, d):
        l = levels - 1 - step
        pieces = dot3(d, (wh[l - 1], wl[l - 1]), NN)
        sources = [tdep[j, l - 1] for j in range(dep)]
        for slot in range(slots):
            total = None
            for j in range(dep):
                term = jnp.where(sources[j] == slot, 1.0, 0.0) * pieces[:, j * s:(j + 1) * s]
                total = term if total is None else total + term
            bout[l - 1, slot] = total
        for slot, device in row_out:
            b_copy(l - 1, slot, n_col + me_r, device).start()
        for slot, device in col_out:
            b_copy(l - 1, slot, me_c, device).start()
        bin_[l - 1, me_c] = bout[l - 1, me_c]
        bin_[l - 1, n_col + me_r] = bout[l - 1, n_col + me_r]
        publish(l, d)
        for extra in range(per_gap):
            local_fold(early + step * per_gap + extra)
        for slot, device in col_out + row_out:
            b_copy(l - 1, slot, slot, device).wait_recv()
        total = bin_[l - 1, 0]
        for slot in range(1, slots):
            total = total + bin_[l - 1, slot]
        return yown[l - 1] - total

    d = lax.fori_loop(0, levels - 1, backward, d)
    publish(0, d)

    def ag_wait(l, carry):
        for p, device in zip(leaf_peers, at_leaf):
            ag_copy(l, p, p, device).wait_recv()
        return carry

    lax.fori_loop(0, levels, ag_wait, 0)
    top_out = pltpu.make_async_copy(tsol, tsol_h, out_sem.at[n_chunks])
    top_out.start()

    outs = []
    for c in range(n_chunks):
        ks = pl.ds(c * chunk, chunk)
        for k in range(c * chunk, (c + 1) * chunk):
            above = jnp.concatenate([tsol[ldep[j, k]] for j in range(fan)], axis=1)
            lsol[k] = first[k] - dot3(above, (vh[k], vl[k]), NN)
        outs.append(pltpu.make_async_copy(lsol.at[ks], lsol_h.at[ks], out_sem.at[c]))
        outs[-1].start()

    for half in range(2):
        for p, device in zip(leaf_peers, at_leaf):
            rs_copy(half, p, q, device).wait_send()

    def drain(l, carry):
        for target in row_out:
            f_copy(l, n_col + me_r, target).wait_send()
        for target in col_out:
            f_copy(l, me_c, target).wait_send()
        for slot, device in row_out + col_out:
            b_copy(l, slot, slot, device).wait_send()
        return carry

    lax.fori_loop(0, levels - 1, drain, 0)

    def drain_ag(l, carry):
        for p, device in zip(leaf_peers, at_leaf):
            ag_copy(l, p, q, device).wait_send()
        return carry

    lax.fori_loop(0, levels, drain_ag, 0)
    for out in outs + [top_out]:
        out.wait()


def on_device(sizes, local_inv, local_off, local_dep, local_rhs, top_inv, top_off, top_dep, top_rhs):
    n_leaf, n_row, n_col = sizes
    loc, s = local_inv.shape[2], local_inv.shape[3]
    fan = local_off.shape[3]
    r = local_rhs.shape[3]
    levels, dep = top_inv.shape[0], top_off.shape[3]
    part, slots = r // n_leaf, n_row + n_col
    chunk = 4 if loc % 4 == 0 else 1
    n_chunks = loc // chunk
    hbm = pl.BlockSpec(memory_space=pl.ANY)
    smem = pl.BlockSpec(memory_space=pltpu.SMEM)
    dma = pltpu.SemaphoreType.DMA
    local_sol, top_sol = pl.pallas_call(
        functools.partial(kernel, sizes, chunk),
        out_shape=(
            jax.ShapeDtypeStruct((loc, r, s), f32),
            jax.ShapeDtypeStruct((levels, r, s), f32),
        ),
        in_specs=[smem, smem] + [hbm] * 6,
        out_specs=(hbm, hbm),
        scratch_shapes=[
            pltpu.VMEM((loc, s, s), f32),
            pltpu.VMEM((loc, fan * s, s), f32),
            pltpu.VMEM((loc, r, s), f32),
            pltpu.VMEM((levels, s, s), f32),
            pltpu.VMEM((levels - 1, dep * s, s), f32),
            pltpu.VMEM((levels, part, s), f32),
            pltpu.VMEM((loc, r, s), f32),
            pltpu.VMEM((levels, r, s), f32),
            pltpu.VMEM((n_leaf, levels, part, s), f32),
            pltpu.VMEM((levels - 1, slots, part, s), f32),
            pltpu.VMEM((levels, part, s), f32),
            pltpu.VMEM((levels - 1, slots, part, s), f32),
            pltpu.VMEM((levels - 1, slots, part, s), f32),
            pltpu.VMEM((levels, r, s), f32),
            pltpu.VMEM((loc, r, s), f32),
            pltpu.VMEM((levels - 1, s, dep * s), bf16),
            pltpu.VMEM((levels - 1, s, dep * s), bf16),
            pltpu.VMEM((loc, fan * s, s), bf16),
            pltpu.VMEM((loc, fan * s, s), bf16),
            dma((3 * n_chunks + 3,)),
            dma((n_chunks + 1,)),
            dma((2, n_leaf)),
            dma((2, n_leaf)),
            dma((levels - 1, slots)),
            dma((levels - 1, slots)),
            dma((levels - 1, slots)),
            dma((levels - 1, slots)),
            dma((levels, n_leaf)),
            dma((levels, n_leaf)),
        ],
        compiler_params=pltpu.CompilerParams(
            collective_id=0, has_side_effects=True, vmem_limit_bytes=62 * 2**20
        ),
    )(
        local_dep.reshape(loc, fan).T,
        top_dep.reshape(levels - 1, dep).T,
        local_inv.reshape(loc, s, s),
        local_off.reshape(loc, fan * s, s),
        local_rhs.reshape(loc, r, s),
        top_inv.reshape(levels, s, s),
        top_off.reshape(levels - 1, dep * s, s),
        top_rhs.reshape(levels, r, s),
    )
    return local_sol[None, None], top_sol[:, None, None]


def solution(mesh):
    placed = (
        P("leaf", "row", "col", None, None),
        P("leaf", "row", "col", None, None, None),
        P("leaf", "row", "col", None),
        P("leaf", "row", "col", None, None),
        P(None, "row", "col", None, None),
        P(None, "row", "col", None, None, None),
        P(None, "row", "col", None),
        P(None, "row", "col", None, None),
    )
    sizes = (mesh.shape["leaf"], mesh.shape["row"], mesh.shape["col"])
    return jax.shard_map(
        functools.partial(on_device, sizes),
        mesh=mesh,
        in_specs=placed,
        out_specs=(P("leaf", "row", "col", None, None), P(None, "row", "col", None, None)),
        check_vma=False,
    )
```

```python
import functools

import jax
import jax.numpy as jnp
from jax import lax
from jax.experimental import pallas as pl
from jax.experimental.pallas import tpu as pltpu
from jax.sharding import PartitionSpec as P

MESH = pl.DeviceIdType.MESH
f32 = jnp.float32
bf16 = jnp.bfloat16
NN = (((1,), (0,)), ((), ()))
NT = (((1,), (1,)), ((), ()))


def split(x):
    high = x.astype(bf16)
    return high, (x - high.astype(f32)).astype(bf16)


def dot3(a, b, dims):
    rows = a.shape[0]
    ah, al = split(a)
    bh, bl = b
    both = lax.dot_general(jnp.concatenate([ah, al], axis=0), bh, dims, preferred_element_type=f32)
    cross = lax.dot_general(ah, bl, dims, preferred_element_type=f32)
    return both[:rows] + both[rows:] + cross


def farthest_first(me, n):
    upper = (2 * me) // n
    peers = []
    for i in range(n - 1):
        up = i + jnp.where(i >= me, 1, 0)
        down = n - 1 - i - jnp.where(n - 1 - i <= me, 1, 0)
        peers.append(upper * up + (1 - upper) * down)
    return peers


def kernel(
    sizes, chunk,
    ldep, tdep, inv_h, off_h, rhs_h, tinv_h, toff_h, trhs_h,
    lsol_h, tsol_h,
    inv, off, rhs, tinv, toff, trhs, first, upd, rs, ybuf, yown, bout, bin_, tsol, lsol,
    wh, wl, vh, vl,
    in_sem, out_sem, rs_send, rs_recv, f_send, f_recv, b_send, b_recv, ag_send, ag_recv,
):
    n_leaf, n_row, n_col = sizes
    loc, s = inv.shape[0], inv.shape[1]
    fan = off.shape[1] // s
    levels, r = upd.shape[0], upd.shape[1]
    dep = tdep.shape[0]
    part = r // n_leaf
    slots = n_col + n_row
    q, me_r, me_c = lax.axis_index("leaf"), lax.axis_index("row"), lax.axis_index("col")
    leaf_peers = [lax.rem(q + d, n_leaf) for d in range(1, n_leaf)]
    row_peers = farthest_first(me_r, n_row)
    col_peers = [lax.rem(me_c + d, n_col) for d in range(1, n_col)]
    at_leaf = [(p, me_r, me_c) for p in leaf_peers]
    at_row = [(q, p, me_c) for p in row_peers]
    at_col = [(q, me_r, p) for p in col_peers]

    def rows_of(p):
        return pl.ds(pl.multiple_of(p * part, part), part)

    mine = rows_of(q)

    n_chunks = loc // chunk
    loads = []
    for c in range(n_chunks):
        ks = pl.ds(c * chunk, chunk)
        for place, (src, dst) in enumerate(((rhs_h, rhs), (inv_h, inv), (off_h, off))):
            loads.append(pltpu.make_async_copy(src.at[ks], dst.at[ks], in_sem.at[3 * c + place]))
    late = 3 * n_chunks
    top_loads = [
        pltpu.make_async_copy(tinv_h, tinv, in_sem.at[late]),
        pltpu.make_async_copy(trhs_h.at[:, mine], trhs, in_sem.at[late + 1]),
        pltpu.make_async_copy(toff_h, toff, in_sem.at[late + 2]),
    ]
    for load in loads + top_loads:
        load.start()

    barrier = pltpu.get_barrier_semaphore()
    for peer in at_leaf + at_row + at_col:
        pl.semaphore_signal(barrier, inc=1, device_id=peer, device_id_type=MESH)

    for c in range(n_chunks):
        for load in loads[3 * c:3 * c + 3]:
            load.wait()
        contributions = []
        for k in range(c * chunk, (c + 1) * chunk):
            y = dot3(rhs[k], split(inv[k]), NT)
            first[k] = y
            both = dot3(y, split(off[k]), NT)
            for j in range(fan):
                contributions.append((ldep[j, k], both[:, j * s:(j + 1) * s]))
        for l in range(levels):
            total = None
            for level, block in contributions:
                term = jnp.where(level == l, 1.0, 0.0) * block
                total = term if total is None else total + term
            upd[l] = total if c == 0 else upd[l] + total

    pl.semaphore_wait(barrier, n_leaf + n_row + n_col - 3)

    def rs_copy(half, p, slot, device):
        ls = pl.ds(0, 1) if half == 0 else pl.ds(1, levels - 1)
        return pltpu.make_async_remote_copy(
            src_ref=upd.at[ls, rows_of(p)], dst_ref=rs.at[slot, ls],
            send_sem=rs_send.at[half, p], recv_sem=rs_recv.at[half, slot],
            device_id=device, device_id_type=MESH,
        )

    for half in range(2):
        for p, device in zip(leaf_peers, at_leaf):
            rs_copy(half, p, q, device).start()
    rs[q] = upd[:, mine]

    def local_fold(k):
        both = dot3(jnp.concatenate([off[k], first[k]], axis=0), split(inv[k]), NN)
        high, low = split(both[:fan * s])
        vh[k] = high
        vl[k] = low
        first[k] = both[fan * s:]

    for load in top_loads:
        load.wait()
    per_gap = loc // (levels - 1)
    early = loc - per_gap * (levels - 1)
    for k in range(early):
        local_fold(k)

    def rs_wait(half):
        for p, device in zip(leaf_peers, at_leaf):
            rs_copy(half, p, p, device).wait_recv()

    def own_part(l):
        z = trhs[l]
        for p in range(n_leaf):
            z = z - rs[p, l]
        return dot3(z, split(tinv[l]), NT)

    def f_copy(l, slot, device):
        return pltpu.make_async_remote_copy(
            src_ref=ybuf.at[l, slot], dst_ref=ybuf.at[l, slot],
            send_sem=f_send.at[l, device[0]], recv_sem=f_recv.at[l, slot],
            device_id=device[1], device_id_type=MESH,
        )

    col_out = [(p, d) for p, d in zip(col_peers, at_col)]
    row_out = [(n_col + p, d) for p, d in zip(row_peers, at_row)]

    def f_start(l, y):
        ybuf[l, me_c] = y
        ybuf[l, n_col + me_r] = y
        for target in row_out:
            f_copy(l, n_col + me_r, target).start()
        for target in col_out:
            f_copy(l, me_c, target).start()

    rs_wait(0)
    y = own_part(0)
    yown[0] = y
    f_start(0, y)
    rs_wait(1)

    def fold(l):
        inverse = tinv[l]
        for j in range(dep):
            high, low = split(dot3(inverse, split(toff[l - 1, j * s:(j + 1) * s]), NN))
            wh[l - 1, :, j * s:(j + 1) * s] = high
            wl[l - 1, :, j * s:(j + 1) * s] = low

    def up(l, y):
        fold(l)
        own = own_part(l)
        picks = [
            [jnp.where(tdep[j, l - 1] == slot, 1.0, 0.0) for slot in range(slots)]
            for j in range(dep)
        ]
        for slot, device in col_out + row_out:
            f_copy(l - 1, slot, (slot, device)).wait_recv()
        blocks = [ybuf[l - 1, slot] for slot in range(slots)]
        picked = []
        for j in range(dep):
            total = None
            for slot in range(slots):
                term = picks[j][slot] * blocks[slot]
                total = term if total is None else total + term
            picked.append(total)
        return own - dot3(jnp.concatenate(picked, axis=1), (wh[l - 1], wl[l - 1]), NT)

    def forward(l, y):
        y = up(l, y)
        yown[l] = y
        f_start(l, y)
        return y

    y = lax.fori_loop(1, levels - 1, forward, y)
    d = up(levels - 1, y)

    def ag_copy(l, p, owner, device):
        return pltpu.make_async_remote_copy(
            src_ref=tsol.at[l, rows_of(owner)], dst_ref=tsol.at[l, rows_of(owner)],
            send_sem=ag_send.at[l, p], recv_sem=ag_recv.at[l, owner],
            device_id=device, device_id_type=MESH,
        )

    def publish(l, d):
        tsol[l, mine] = dot3(d, split(tinv[l]), NN)
        for p, device in zip(leaf_peers, at_leaf):
            ag_copy(l, p, q, device).start()

    def b_copy(l, slot, landing, device):
        return pltpu.make_async_remote_copy(
            src_ref=bout.at[l, slot], dst_ref=bin_.at[l, landing],
            send_sem=b_send.at[l, slot], recv_sem=b_recv.at[l, landing],
            device_id=device, device_id_type=MESH,
        )

    def backward(step, d):
        l = levels - 1 - step
        pieces = dot3(d, (wh[l - 1], wl[l - 1]), NN)
        sources = [tdep[j, l - 1] for j in range(dep)]
        for slot in range(slots):
            total = None
            for j in range(dep):
                term = jnp.where(sources[j] == slot, 1.0, 0.0) * pieces[:, j * s:(j + 1) * s]
                total = term if total is None else total + term
            bout[l - 1, slot] = total
        for slot, device in row_out:
            b_copy(l - 1, slot, n_col + me_r, device).start()
        for slot, device in col_out:
            b_copy(l - 1, slot, me_c, device).start()
        bin_[l - 1, me_c] = bout[l - 1, me_c]
        bin_[l - 1, n_col + me_r] = bout[l - 1, n_col + me_r]
        publish(l, d)
        for extra in range(per_gap):
            local_fold(early + step * per_gap + extra)
        for slot, device in col_out + row_out:
            b_copy(l - 1, slot, slot, device).wait_recv()
        total = bin_[l - 1, 0]
        for slot in range(1, slots):
            total = total + bin_[l - 1, slot]
        return yown[l - 1] - total

    d = lax.fori_loop(0, levels - 1, backward, d)
    publish(0, d)

    def ag_wait(l, carry):
        for p, device in zip(leaf_peers, at_leaf):
            ag_copy(l, p, p, device).wait_recv()
        return carry

    lax.fori_loop(0, levels, ag_wait, 0)
    top_out = pltpu.make_async_copy(tsol, tsol_h, out_sem.at[n_chunks])
    top_out.start()

    outs = []
    for c in range(n_chunks):
        ks = pl.ds(c * chunk, chunk)
        for k in range(c * chunk, (c + 1) * chunk):
            above = jnp.concatenate([tsol[ldep[j, k]] for j in range(fan)], axis=1)
            lsol[k] = first[k] - dot3(above, (vh[k], vl[k]), NN)
        outs.append(pltpu.make_async_copy(lsol.at[ks], lsol_h.at[ks], out_sem.at[c]))
        outs[-1].start()

    for half in range(2):
        for p, device in zip(leaf_peers, at_leaf):
            rs_copy(half, p, q, device).wait_send()

    def drain(l, carry):
        for target in row_out:
            f_copy(l, n_col + me_r, target).wait_send()
        for target in col_out:
            f_copy(l, me_c, target).wait_send()
        for slot, device in row_out + col_out:
            b_copy(l, slot, slot, device).wait_send()
        return carry

    lax.fori_loop(0, levels - 1, drain, 0)

    def drain_ag(l, carry):
        for p, device in zip(leaf_peers, at_leaf):
            ag_copy(l, p, q, device).wait_send()
        return carry

    lax.fori_loop(0, levels, drain_ag, 0)
    for out in outs + [top_out]:
        out.wait()


def hand_out(local_h, top_h, local_o, top_o, local_v, top_v, in_sem, out_sem):
    half = local_v.shape[0] // 2
    steps = []
    for i, (src, mid, dst) in enumerate((
        (local_h.at[:half], local_v.at[:half], local_o.at[:half]),
        (local_h.at[half:], local_v.at[half:], local_o.at[half:]),
        (top_h, top_v, top_o),
    )):
        steps.append((
            pltpu.make_async_copy(src, mid, in_sem.at[i]),
            pltpu.make_async_copy(mid, dst, out_sem.at[i]),
        ))
    for load, _ in steps:
        load.start()
    for load, store in steps:
        load.wait()
        store.start()
    for _, store in steps:
        store.wait()


def on_device(sizes, local_inv, local_off, local_dep, local_rhs, top_inv, top_off, top_dep, top_rhs):
    n_leaf, n_row, n_col = sizes
    loc, s = local_inv.shape[2], local_inv.shape[3]
    fan = local_off.shape[3]
    r = local_rhs.shape[3]
    levels, dep = top_inv.shape[0], top_off.shape[3]
    part, slots = r // n_leaf, n_row + n_col
    chunk = 4 if loc % 4 == 0 else 1
    n_chunks = loc // chunk
    hbm = pl.BlockSpec(memory_space=pl.ANY)
    smem = pl.BlockSpec(memory_space=pltpu.SMEM)
    dma = pltpu.SemaphoreType.DMA
    local_sol, top_sol = pl.pallas_call(
        functools.partial(kernel, sizes, chunk),
        out_shape=(
            jax.ShapeDtypeStruct((loc, r, s), f32),
            jax.ShapeDtypeStruct((levels, r, s), f32),
        ),
        in_specs=[smem, smem] + [hbm] * 6,
        out_specs=(hbm, hbm),
        scratch_shapes=[
            pltpu.VMEM((loc, s, s), f32),
            pltpu.VMEM((loc, fan * s, s), f32),
            pltpu.VMEM((loc, r, s), f32),
            pltpu.VMEM((levels, s, s), f32),
            pltpu.VMEM((levels - 1, dep * s, s), f32),
            pltpu.VMEM((levels, part, s), f32),
            pltpu.VMEM((loc, r, s), f32),
            pltpu.VMEM((levels, r, s), f32),
            pltpu.VMEM((n_leaf, levels, part, s), f32),
            pltpu.VMEM((levels - 1, slots, part, s), f32),
            pltpu.VMEM((levels, part, s), f32),
            pltpu.VMEM((levels - 1, slots, part, s), f32),
            pltpu.VMEM((levels - 1, slots, part, s), f32),
            pltpu.VMEM((levels, r, s), f32),
            pltpu.VMEM((loc, r, s), f32),
            pltpu.VMEM((levels - 1, s, dep * s), bf16),
            pltpu.VMEM((levels - 1, s, dep * s), bf16),
            pltpu.VMEM((loc, fan * s, s), bf16),
            pltpu.VMEM((loc, fan * s, s), bf16),
            dma((3 * n_chunks + 3,)),
            dma((n_chunks + 1,)),
            dma((2, n_leaf)),
            dma((2, n_leaf)),
            dma((levels - 1, slots)),
            dma((levels - 1, slots)),
            dma((levels - 1, slots)),
            dma((levels - 1, slots)),
            dma((levels, n_leaf)),
            dma((levels, n_leaf)),
        ],
        compiler_params=pltpu.CompilerParams(
            collective_id=0, has_side_effects=True, vmem_limit_bytes=62 * 2**20
        ),
    )(
        local_dep.reshape(loc, fan).T,
        top_dep.reshape(levels - 1, dep).T,
        local_inv.reshape(loc, s, s),
        local_off.reshape(loc, fan * s, s),
        local_rhs.reshape(loc, r, s),
        top_inv.reshape(levels, s, s),
        top_off.reshape(levels - 1, dep * s, s),
        top_rhs.reshape(levels, r, s),
    )
    local_sol, top_sol = pl.pallas_call(
        hand_out,
        out_shape=(
            jax.ShapeDtypeStruct((loc, r, s), f32),
            jax.ShapeDtypeStruct((levels, r, s), f32),
        ),
        in_specs=[hbm, hbm],
        out_specs=(hbm, hbm),
        scratch_shapes=[
            pltpu.VMEM((loc, r, s), f32),
            pltpu.VMEM((levels, r, s), f32),
            dma((3,)),
            dma((3,)),
        ],
        compiler_params=pltpu.CompilerParams(vmem_limit_bytes=62 * 2**20),
    )(local_sol, top_sol)
    return local_sol[None, None], top_sol[:, None, None]


def solution(mesh):
    placed = (
        P("leaf", "row", "col", None, None),
        P("leaf", "row", "col", None, None, None),
        P("leaf", "row", "col", None),
        P("leaf", "row", "col", None, None),
        P(None, "row", "col", None, None),
        P(None, "row", "col", None, None, None),
        P(None, "row", "col", None),
        P(None, "row", "col", None, None),
    )
    sizes = (mesh.shape["leaf"], mesh.shape["row"], mesh.shape["col"])
    return jax.shard_map(
        functools.partial(on_device, sizes),
        mesh=mesh,
        in_specs=placed,
        out_specs=(P("leaf", "row", "col", None, None), P(None, "row", "col", None, None)),
        check_vma=False,
    )
```
